32 devices in a mesh: rep: 2 (over x), expert: 8 (over z, y), head: 2 (over core).
Axes of the slice: x: 2, y: 2, z: 4, core: 2. Of those that a mesh axis runs over, the one named last changes fastest.
Arguments:
- hidden_in: bfloat16 [256, 3072], P('rep', ('expert', 'head')), parts along dimension 0, may hold values from -7 to 7
- queries: bfloat16 [256, 4, 6, 128], P(('rep', 'expert'), 'head'), parts along dimension 0, may hold values from -18 to 18, as said below
- new_keys: bfloat16 [256, 4, 128], P(('rep', 'expert'), 'head'), parts along dimension 0, may hold values from -4 to 4
- new_values: bfloat16 [256, 4, 128], P(('rep', 'expert'), 'head'), parts along dimension 0, may hold values from -4 to 4
- cache_keys: bfloat16 [256, 4, 64, 128], P(('rep', 'expert'), 'head'), parts along dimension 0, may hold values from -18 to 18, as said below
- cache_values: bfloat16 [256, 4, 64, 128], P(('rep', 'expert'), 'head'), parts along dimension 0, may hold values from -4 to 4
- parents: int32 [256], P(('rep', 'expert')), parts along dimension 0, may hold values from 0 to 7
- lengths: int32 [32], P(('rep', 'expert')), parts along dimension 0, may hold values from 2 to 64, as said below
- out_proj: bfloat16 [3072, 3072], P(None, ('expert', 'head')), may hold values from -0.109375 to 0.109375
- ffn_gain: float32 [3072], replicated, may hold values from 0.1 to 1.9
- routes: int32 [256, 2], P('rep'), parts along dimension 0, may hold values from 0 to 3, all different within a row; in each aligned block of 128 rows (0 to 127, 128 to 255, ...) at most 80 rows name the same one
- route_weights: float32 [256, 2], P('rep'), parts along dimension 0, may hold values from 0.2 to 1
- w_gate: bfloat16 [3072, 32768], P(None, ('expert', 'head')), may hold values from -0.109375 to 0.109375
- w_up: bfloat16 [3072, 32768], P(None, ('expert', 'head')), may hold values from -0.109375 to 0.109375
- w_down: bfloat16 [32768, 3072], P(('expert', 'head')), may hold values from -0.0625 to 0.0625
- lm_gain: float32 [3072], replicated, may hold values from 0.1 to 1.9
- vocab_weight: bfloat16 [3072, 16384], P(None, ('expert', 'head')), may hold values from -1 to 1
Outputs:
- layer_out: bfloat16 [256, 3072], P('rep', ('expert', 'head')), parts along dimension 0
- best_logits: float32 [256, 8], P('rep'), parts along dimension 0
The draws below stay inside these ranges and needn't reach their ends.
There are 2 independent parts, one for each index of `rep`. The reference program is written for one: setup_inputs(seed, part) draws one part's arguments, and reference() takes and returns one part's arrays. A program takes and returns all parts, laid end to end along the dimension named above; an argument that names none is the same for every part. Nothing has to cross between parts.
Inputs may be any that keep to these rules, and one draw needn't show every extreme that they name: `queries`: in the shown draw entries are truncated normal; values always lie in the printed range. `cache_keys`: in the shown draw entries are truncated normal; values always lie in the printed range. `lengths`: some sequence has exactly 64 cached positions. `routes`: each row names two different experts; no expert is named by more than 80 rows, and one is named by exactly 80.
All inputs are finite; a program needn't handle non-finite values.
Results may differ from the reference program's by a relative error of at most 0.0065.
Values may be sent and summed in bfloat16 or wider, within the bound.
A program may use at most 128 MiB of HBM per device.

```python
import math
import jax
import jax.numpy as jnp
import numpy as np
from jax import lax

D = 3072
HQ = 24
KVH = 4
HD = 128
E = 4
FF = 8192
V = 16384
BEAM = 8
TOPK = 8
CACHE = 64
ROWS = 128
SEQS = 16
CAP = 80
GROUP = 6
SLICES = 4
N_EXPERT = 8
N_HEAD = 2


def feature_direction():
    positions = jnp.arange(D, dtype=jnp.float32)
    return math.sqrt(2.0) * jnp.cos(2.399963 * positions + 0.5)


def draw_hidden_in(key, part):
    key = jax.random.fold_in(key, 41)
    noise = jax.random.truncated_normal(key, -4.0, 4.0, (ROWS, D), jnp.float32)
    strength = jnp.where(jnp.arange(ROWS) % 2 == 0, 1.5, 0.0).astype(jnp.float32)
    return (noise + strength[:, None] * feature_direction()[None, :]).astype(jnp.bfloat16)


def draw_vocab_weight(key, part):
    key = jax.random.fold_in(key, 53)
    noise_key, block_key, grade_key = jax.random.split(key, 3)
    scale = 1.0 / math.sqrt(D)
    noise = jax.random.truncated_normal(noise_key, -4.0, 4.0, (D, V), jnp.float32) * scale
    block_width = V // (N_EXPERT * N_HEAD)
    half_width = block_width // 2
    block_index = jax.random.randint(block_key, (), 0, N_EXPERT * N_HEAD, jnp.int32)
    offsets = jnp.array([0, 1, 2, 3, half_width, half_width + 1, half_width + 2, half_width + 3], jnp.int32)
    columns = block_index * block_width + offsets
    grades = 8.0 + 0.7 * jnp.arange(8, dtype=jnp.float32) + 0.3 * jax.random.uniform(grade_key, (8,), jnp.float32)
    lift = feature_direction()[:, None] * grades[None, :] / D
    return noise.at[:, columns].add(lift).astype(jnp.bfloat16)


def draw_queries(key, part):
    key = jax.random.fold_in(key, 11)
    values = jax.random.truncated_normal(key, -4.0, 4.0, (ROWS, KVH, GROUP, HD), jnp.float32)
    return values.astype(jnp.bfloat16)


def draw_cache_keys(key, part):
    key = jax.random.fold_in(key, 23)
    values = jax.random.truncated_normal(key, -4.0, 4.0, (ROWS, KVH, CACHE, HD), jnp.float32)
    return values.astype(jnp.bfloat16)


def draw_lengths(key, part):
    key = jax.random.fold_in(key, 37)
    drawn = jax.random.randint(key, (SEQS,), 2, CACHE + 1, jnp.int32)
    return drawn.at[0].set(CACHE)


def with_ends(values, stream_key, smallest, largest):
    dims = values.shape
    place = [jax.random.randint(jax.random.fold_in(stream_key, axis), (), 0, dims[axis]) for axis in range(len(dims))]
    values = values.at[tuple(place)].set(smallest)
    longest = dims.index(max(dims))
    place[longest] = (place[longest] + 1) % dims[longest]
    return values.at[tuple(place)].set(largest)


def levels(rng, shape, cuts, smallest, largest):
    factor_of = 1.0
    for position, parts in cuts:
        heights = jax.random.uniform(jax.random.fold_in(jax.random.fold_in(rng, 6), position), (parts,), jnp.float32, smallest / len(cuts), largest / len(cuts))
        factor_of = factor_of * jnp.repeat(jnp.exp(heights), shape[position] // parts).reshape((-1,) + (1,) * (len(shape) - 1 - position))
    return factor_of


def routed_block(own_key, own, number, rows, count, top, bound, skew):
    sequence = jax.random.permutation(own_key, count)
    heavy_load, usual = shares(count, rows * top, bound, skew, True), shares(count, rows * top, bound, skew, False)
    places = jnp.arange(count)

    def named(tallies, turn):
        used = int((tallies > 0).sum())
        fixed = max(1, used // 4)
        shifted = fixed + (places - fixed + turn * (used - fixed)) % max(1, count - fixed)
        return jnp.zeros((count,), jnp.int32).at[sequence[jnp.where(places < fixed, places, shifted)]].set(jnp.asarray(tallies, jnp.int32))

    tallies = jnp.where(number % 4 == 0, named(heavy_load, number // 4), named(usual, number - number // 4 - 1))
    mixed = jax.random.permutation(jax.random.fold_in(own, 3), count)
    donor, receiver = mixed[0:count // 2 * 2:2], mixed[1:count // 2 * 2:2]
    slack = jnp.minimum(tallies[donor] - 1, bound - tallies[receiver]) // 2
    slack = jnp.where((donor == sequence[0]) | (receiver == sequence[0]) | (tallies[receiver] == 0), 0, jnp.maximum(slack, 0))
    shifted = jax.random.randint(jax.random.fold_in(own, 4), (count // 2,), 0, 1 << 20) % (slack + 1)
    tallies = tallies.at[donor].add(-shifted).at[receiver].add(shifted)
    labels = jnp.searchsorted(jnp.cumsum(tallies), jnp.arange(rows * top), side="right").astype(jnp.int32)
    grid = labels.reshape(top, rows).T
    grid = grid[jax.random.permutation(jax.random.fold_in(own, 1), rows)]
    turn = jax.random.randint(jax.random.fold_in(own, 2), (rows, 1), 0, top)
    return jnp.take_along_axis(grid, (jnp.arange(top)[None, :] + turn) % top, axis=1)


def shares(amount, total, limit, skew, full):
    loads = [(1 << 20) // math.isqrt(standing ** skew) + 1 for standing in range(1, amount + 1)]
    largest = limit if full else min(limit, max(-(-total // amount), total * loads[0] // sum(loads)))
    least = 1 if total - largest >= amount - 1 else 0
    counts, surplus = [largest] + [least] * (amount - 1), total - largest - least * (amount - 1)
    while surplus > 0:
        free = [i for i in range(1, amount) if counts[i] < largest] or [i for i in range(1, amount) if counts[i] < limit]
        whole, left = sum([loads[i] for i in free]), surplus
        for i in free:
            addition = min(limit - counts[i], max(1, left * loads[i] // whole), surplus)
            counts[i] = counts[i] + addition
            surplus = surplus - addition
    return np.array(counts)


def scatter_about(own_key, shape, spread, bound, shards=(), kind=jnp.bfloat16):
    factor_of = levels(own_key, shape, shards, -0.22, 0.18) if shards else 1.0
    values = jax.random.normal(own_key, shape, jnp.float32) * spread * factor_of
    return jnp.minimum(jnp.maximum(values, -bound), bound).astype(kind)


def setup_inputs(seed: int = 0, part: int = 0) -> dict:
    key_list = jax.random.split(jax.random.key(seed), 18)
    own_keys = jax.random.split(jax.random.fold_in(key_list[17], part), 18)
    hidden_in = draw_hidden_in(jax.random.fold_in(jax.random.fold_in(key_list[17], part), 71), part)
    queries = draw_queries(jax.random.fold_in(jax.random.fold_in(key_list[17], part), 71), part)
    new_keys = scatter_about(own_keys[2], (ROWS, KVH, HD), 1.0, 4.0, ((0, 8), (1, 2)))
    new_values = scatter_about(own_keys[3], (ROWS, KVH, HD), 1.0, 4.0, ((0, 8), (1, 2)))
    cache_keys = draw_cache_keys(jax.random.fold_in(jax.random.fold_in(key_list[17], part), 71), part)
    cache_values = scatter_about(own_keys[5], (ROWS, KVH, CACHE, HD), 1.0, 4.0, ((0, 8), (1, 2)))
    parents = with_ends(jax.random.randint(own_keys[6], (ROWS,), 0, BEAM), jax.random.fold_in(own_keys[6], 1), 0, BEAM - 1).astype(jnp.int32)
    lengths = draw_lengths(jax.random.fold_in(jax.random.fold_in(key_list[17], part), 71), part)
    out_proj = scatter_about(key_list[8], (HQ * HD, D), (HQ * HD) ** -0.5, 0.109375, ((1, 16),))
    ffn_gain = jnp.clip(1.0 + 0.18 * jax.random.normal(key_list[9], (D,), jnp.float32), 0.1, 1.9)
    routes_keys = jax.random.split(jax.random.fold_in(own_keys[10], 1), ROWS // ROWS)
    routes_turns = jax.random.permutation(jax.random.fold_in(own_keys[10], 3), ROWS // ROWS)
    routes = jax.vmap(lambda own, number: routed_block(jax.random.fold_in(own_keys[10], 2), own, number, ROWS, E, 2, CAP, 1))(routes_keys, routes_turns).reshape((ROWS, 2))
    route_weights = jnp.clip(jax.random.uniform(own_keys[11], (ROWS, 2), jnp.float32, 0.2, 1.0), 0.2, 1.0)
    w_gate = scatter_about(key_list[12], (D, E * FF), D ** -0.5, 0.109375, ((1, 16),))
    w_up = scatter_about(key_list[13], (D, E * FF), D ** -0.5, 0.109375, ((1, 16),))
    w_down = scatter_about(key_list[14], (E * FF, D), FF ** -0.5, 0.0625, ((0, 16),))
    lm_gain = jnp.clip(1.0 + 0.18 * jax.random.normal(key_list[15], (D,), jnp.float32), 0.1, 1.9)
    vocab_weight = draw_vocab_weight(jax.random.fold_in(key_list[17], 71), part)
    return dict(hidden_in=hidden_in, queries=queries, new_keys=new_keys, new_values=new_values, cache_keys=cache_keys, cache_values=cache_values, parents=parents, lengths=lengths, out_proj=out_proj, ffn_gain=ffn_gain, routes=routes, route_weights=route_weights, w_gate=w_gate, w_up=w_up, w_down=w_down, lm_gain=lm_gain, vocab_weight=vocab_weight)


def rms_scale(rows, gain):
    values = rows.astype(jnp.float32)
    square_mean = lax.optimization_barrier(jnp.mean(values * values, axis=-1, keepdims=True))
    return (values * lax.rsqrt(square_mean + 1e-05) * gain.astype(jnp.float32)).astype(jnp.bfloat16)

def attend(queries, new_keys, new_values, cache_keys, cache_values, parents, lengths):
    row_count = queries.shape[0]
    beam_base = jnp.arange(row_count, dtype=jnp.int32) // BEAM * BEAM
    source = beam_base + parents.astype(jnp.int32)
    picked_keys = jnp.take(cache_keys, source, axis=0)
    picked_values = jnp.take(cache_values, source, axis=0)
    factor = 1.0 / math.sqrt(queries.shape[-1])
    scores = jnp.einsum('rgjd,rgtd->rgjt', queries.astype(jnp.float32), picked_keys.astype(jnp.float32)) * factor
    fresh_score = jnp.einsum('rgjd,rgd->rgj', queries.astype(jnp.float32), new_keys.astype(jnp.float32)) * factor
    limits = jnp.repeat(lengths.astype(jnp.int32), BEAM)
    in_cache = jnp.arange(cache_keys.shape[2], dtype=jnp.int32)[None, :] < limits[:, None]
    scores = jnp.where(in_cache[:, None, None, :], scores, -1e+30)
    highest = jnp.maximum(lax.optimization_barrier(jnp.max(scores, axis=-1)), fresh_score)
    expo = jnp.exp(scores - highest[..., None])
    own_term = jnp.exp(fresh_score - highest)
    denominator = lax.optimization_barrier(jnp.sum(expo, axis=-1)) + own_term
    weights = (expo / denominator[..., None]).astype(jnp.bfloat16)
    own_weight = (own_term / denominator).astype(jnp.bfloat16)
    context = jnp.einsum('rgjt,rgtd->rgjd', weights.astype(jnp.float32), picked_values.astype(jnp.float32))
    context = context + own_weight.astype(jnp.float32)[..., None] * new_values.astype(jnp.float32)[:, :, None, :]
    return context.astype(jnp.bfloat16).reshape(row_count, -1)

def place_slots(routes, capacity):
    row_count = routes.shape[0]
    flat_expert = routes.reshape(-1).astype(jnp.int32)
    onehot = (flat_expert[:, None] == jnp.arange(E, dtype=jnp.int32)[None, :]).astype(jnp.int32)
    before = jnp.cumsum(onehot, axis=0) - onehot
    slot_index = lax.optimization_barrier(jnp.sum(before * onehot, axis=1)).astype(jnp.int32)
    row_ids = jnp.arange(2 * row_count, dtype=jnp.int32) // 2
    slot_table = jnp.full((E, capacity), row_count, jnp.int32).at[flat_expert, slot_index].set(row_ids)
    return (flat_expert, slot_index, slot_table)

def reference(hidden_in, queries, new_keys, new_values, cache_keys, cache_values, parents, lengths, out_proj, ffn_gain, routes, route_weights, w_gate, w_up, w_down, lm_gain, vocab_weight):
    context = attend(queries, new_keys, new_values, cache_keys, cache_values, parents, lengths)
    attention = jnp.dot(context, out_proj, preferred_element_type=jnp.float32)
    residual = (hidden_in.astype(jnp.float32) + attention).astype(jnp.bfloat16)
    flat_expert, slot_index, slot_table = place_slots(routes, CAP)
    padded = jnp.concatenate([residual, jnp.zeros((1, D), jnp.bfloat16)], axis=0)
    block_width = FF // SLICES
    outputs = []
    for expert in range(E):
        normed = rms_scale(jnp.take(padded, slot_table[expert], axis=0), ffn_gain)
        gate_proj = jnp.dot(normed, w_gate[:, expert * FF:(expert + 1) * FF], preferred_element_type=jnp.float32)
        up_proj = jnp.dot(normed, w_up[:, expert * FF:(expert + 1) * FF], preferred_element_type=jnp.float32)
        hidden = (jax.nn.silu(gate_proj) * up_proj).astype(jnp.bfloat16)
        down_rows = w_down[expert * FF:(expert + 1) * FF].reshape(SLICES, block_width, D)
        partial_value = jnp.einsum('csf,sfd->scd', hidden.reshape(CAP, SLICES, block_width).astype(jnp.float32), down_rows.astype(jnp.float32))
        outputs.append(lax.optimization_barrier(jnp.sum(partial_value.astype(jnp.bfloat16).astype(jnp.float32), axis=0)))
    expert_out = jnp.stack(outputs, axis=0)
    picked = expert_out[flat_expert, slot_index].reshape(ROWS, 2, D)
    expert_mix = lax.optimization_barrier(jnp.sum(route_weights.astype(jnp.float32)[:, :, None] * picked, axis=1))
    layer_out = (residual.astype(jnp.float32) + expert_mix).astype(jnp.bfloat16)
    final = rms_scale(layer_out, lm_gain)
    logits = jnp.dot(final, vocab_weight, preferred_element_type=jnp.float32)
    best_logits = lax.top_k(logits, TOPK)[0]
    return (layer_out, best_logits)
```

```python
import functools
import math

import jax
import jax.numpy as jnp
from jax import lax
from jax.experimental import pallas as pl
from jax.experimental.pallas import tpu as pltpu
from jax.sharding import PartitionSpec as P

E = 4
BEAM = 8
TOPK = 8


def attend(queries, new_keys, new_values, cache_keys, cache_values, parents, lengths):
    row_count = queries.shape[0]
    beam_base = jnp.arange(row_count, dtype=jnp.int32) // BEAM * BEAM
    source = beam_base + parents
    picked_keys = jnp.take(cache_keys, source, axis=0)
    picked_values = jnp.take(cache_values, source, axis=0)
    factor = 1.0 / math.sqrt(queries.shape[-1])
    scores = (
        jnp.einsum("rgjd,rgtd->rgjt", queries, picked_keys, preferred_element_type=jnp.float32)
        * factor
    )
    fresh_score = (
        jnp.einsum("rgjd,rgd->rgj", queries, new_keys, preferred_element_type=jnp.float32) * factor
    )
    limits = jnp.repeat(lengths, BEAM)
    in_cache = jnp.arange(cache_keys.shape[2], dtype=jnp.int32)[None, :] < limits[:, None]
    scores = jnp.where(in_cache[:, None, None, :], scores, -1e30)
    highest = jnp.maximum(jnp.max(scores, axis=-1), fresh_score)
    expo = jnp.exp(scores - highest[..., None])
    own_term = jnp.exp(fresh_score - highest)
    denominator = jnp.sum(expo, axis=-1) + own_term
    weights = (expo / denominator[..., None]).astype(jnp.bfloat16)
    own_weight = (own_term / denominator).astype(jnp.bfloat16)
    context = jnp.einsum(
        "rgjt,rgtd->rgjd", weights, picked_values, preferred_element_type=jnp.float32
    )
    context = (
        context
        + own_weight.astype(jnp.float32)[..., None] * new_values.astype(jnp.float32)[:, :, None, :]
    )
    return context.astype(jnp.bfloat16).reshape(row_count, -1)


TILE = 256
MESH = pl.DeviceIdType.MESH


def aligned(index, size):
    return pl.ds(pl.multiple_of(index * size, size), size)


def best_of(source, groups, width):
    def insert(group, kept):
        item = source[aligned(group, 8), :]
        result = []
        for level in kept:
            result.append(jnp.maximum(level, item))
            item = jnp.minimum(level, item)
        return tuple(result)

    lowest = jnp.full((8, width), -jnp.inf, jnp.float32)
    kept = list(lax.fori_loop(0, groups, insert, (lowest,) * TOPK))
    lane_class = lax.broadcasted_iota(jnp.int32, (8, width), 0)
    best = []
    for _ in range(TOPK):
        top = jnp.max(kept[0], axis=0, keepdims=True)
        first = jnp.min(jnp.where(kept[0] == top, lane_class, 8), axis=0, keepdims=True)
        taken = lane_class == first
        best.append(top)
        kept = [
            jnp.where(taken, kept[j + 1] if j + 1 < TOPK else lowest, kept[j])
            for j in range(TOPK)
        ]
    return best


def layer_kernel(
    n_expert,
    n_head,
    context_ref,
    proj_ref,
    hidden_ref,
    ffn_gain_ref,
    routes_ref,
    route_weights_ref,
    gate_hbm,
    up_hbm,
    down_hbm,
    lm_gain_ref,
    vocab_hbm,
    layer_ref,
    best_ref,
    gate,
    up,
    down,
    vocab,
    load_sem,
    contexts,
    stream,
    final_stream,
    rows_major,
    hidden,
    partials,
    from_core,
    core_sums,
    from_y,
    y_sums,
    from_z,
    logits,
    candidates,
    send_sem,
    recv_sem,
):
    n_devices = n_expert * n_head
    z_size = n_expert // 2
    e = lax.axis_index("expert")
    h = lax.axis_index("head")
    me = e * n_head + h
    z, y = e // 2, lax.rem(e, 2)
    local_rows = context_ref.shape[0]
    width, rows = hidden_ref.shape
    full_width = width * n_devices
    y_peer = {"expert": z * 2 + 1 - y, "head": h}
    core_peer = {"expert": e, "head": 1 - h}

    loads = [
        pltpu.make_async_copy(source, target, load_sem.at[i])
        for i, (source, target) in enumerate(
            ((gate_hbm, gate), (up_hbm, up), (down_hbm, down), (vocab_hbm, vocab))
        )
    ]
    for load in loads:
        load.start()

    def device(index):
        return {"expert": index // n_head, "head": lax.rem(index, n_head)}

    barrier = pltpu.get_barrier_semaphore()

    def greet(k, carry):
        other = lax.rem(me + k, n_devices)
        pl.semaphore_signal(barrier, inc=1, device_id=device(other), device_id_type=MESH)
        return carry

    lax.fori_loop(1, n_devices, greet, 0)
    pl.semaphore_wait(barrier, n_devices - 1)

    def remote(phase, slot, source, target, device_id):
        return pltpu.make_async_remote_copy(
            src_ref=source,
            dst_ref=target,
            send_sem=send_sem.at[phase, slot],
            recv_sem=recv_sem.at[phase, slot],
            device_id=device_id,
            device_id_type=MESH,
        )

    first_y = z_size - 1
    first_core = 2 * z_size - 1

    def loop(start, stop, step):
        def run(k, carry):
            step(k)
            return carry

        lax.fori_loop(start, stop, run, 0)

    def gather(phase, block):
        def move(slot, expert, head, device_id):
            return remote(phase, slot, block(expert, head), block(expert, head), device_id)

        own = block(e, h)

        def to_z(k):
            target = lax.rem(z + k, z_size) * 2 + y
            move(k - 1, e, h, {"expert": target, "head": h}).start()

        loop(1, z_size, to_z)
        move(first_y, e, h, y_peer).start()
        move(first_core, e, h, core_peer).start()

        def on_z(k):
            expert = lax.rem(z + z_size - k, z_size) * 2 + y
            move(k - 1, expert, h, y_peer).wait_recv()
            move(first_y + k, expert, h, y_peer).start()
            move(first_core + k, expert, h, core_peer).start()

        loop(1, z_size, on_z)

        def on_y(k):
            expert = lax.rem(z + z_size - k, z_size) * 2 + 1 - y
            move(first_y + k, expert, h, y_peer).wait_recv()
            move(first_core + z_size + k, expert, h, core_peer).start()

        loop(0, z_size, on_y)

        def on_core(k):
            move(first_core + k, e, 1 - h, core_peer).wait_recv()

        loop(0, 2 * z_size, on_core)

        def sent(k):
            move(k, e, h, core_peer).wait_send()

        loop(0, n_devices - 1, sent)

    def context_block(expert, head):
        return contexts.at[head, aligned(expert, local_rows)]

    def feature_block(buffer):
        return lambda expert, head: buffer.at[aligned(expert * n_head + head, width)]

    contexts[h, aligned(e, local_rows), :] = context_ref[...]
    gather(0, context_block)
    half = context_ref.shape[1]
    attention = hidden_ref[...].astype(jnp.float32)
    for head in range(n_head):
        attention += lax.dot_general(
            proj_ref[:, head * half : (head + 1) * half],
            contexts[head],
            (((1,), (1,)), ((), ())),
            preferred_element_type=jnp.float32,
        )
    residual = attention.astype(jnp.bfloat16)
    stream[aligned(me, width), :] = residual
    gather(1, feature_block(stream))

    def normalise(source, gain_ref):
        def square(i, total):
            block = source[aligned(i, TILE), :].astype(jnp.float32)
            return total + jnp.sum(block * block, axis=0, keepdims=True)

        total = lax.fori_loop(0, full_width // TILE, square, jnp.zeros((1, rows), jnp.float32))
        scale = lax.rsqrt(total / full_width + 1e-05)

        def turn(i):
            block = source[aligned(i, TILE), :].astype(jnp.float32) * scale
            block = block.T * gain_ref[:, aligned(i, TILE)]
            rows_major[:, aligned(i, TILE)] = block.astype(jnp.bfloat16)

        loop(0, full_width // TILE, turn)

    normalise(stream, ffn_gain_ref)
    loads[0].wait()
    loads[1].wait()

    def widen(i):
        columns = aligned(i, TILE)
        normed = rows_major[...]
        gate_proj = jnp.dot(normed, gate[:, columns], preferred_element_type=jnp.float32)
        up_proj = jnp.dot(normed, up[:, columns], preferred_element_type=jnp.float32)
        active = gate_proj / (1.0 + jnp.exp(-gate_proj)) * up_proj
        hidden[:, columns] = active.astype(jnp.bfloat16)

    loop(0, hidden.shape[1] // TILE, widen)
    loads[2].wait()
    expert_here = me // (n_devices // E)
    share = jnp.sum(
        jnp.where(routes_ref[...] == expert_here, route_weights_ref[...], 0.0),
        axis=0,
        keepdims=True,
    )

    def narrow(i):
        columns = aligned(i, TILE)
        product = jnp.dot(hidden[...], down[:, columns], preferred_element_type=jnp.float32)
        partials[columns, :] = (product.T * share).astype(jnp.bfloat16)

    loop(0, full_width // TILE, narrow)

    mine = feature_block(partials)

    def core_copy(expert):
        return remote(
            2, first_core + expert, mine(expert, 1 - h), from_core.at[expert], core_peer
        )

    def y_copy(k):
        return remote(2, first_y + k, core_sums.at[k * 2 + 1 - y], from_y.at[k], y_peer)

    def z_copy(k):
        target = lax.rem(z + k, z_size)
        return remote(
            2,
            k - 1,
            y_sums.at[target],
            from_z.at[k - 1],
            {"expert": target * 2 + y, "head": h},
        )

    def core_order(k):
        turned = lax.rem(z + 1 + lax.rem(k, z_size), z_size)
        side = k // z_size
        return turned, turned * 2 + lax.rem(1 - y + side, 2)

    def core_start(k):
        core_copy(core_order(k)[1]).start()

    loop(0, n_expert, core_start)

    def core_add(expert):
        core_copy(expert).wait_recv()
        own = partials[aligned(expert * n_head + h, width), :].astype(jnp.float32)
        core_sums[expert] = (own + from_core[expert].astype(jnp.float32)).astype(jnp.bfloat16)

    def core_send(k):
        turned, expert = core_order(k)
        core_add(expert)
        y_copy(turned).start()

    loop(0, z_size, core_send)

    def core_keep(k):
        core_add(core_order(k)[1])

    loop(z_size, n_expert, core_keep)

    def y_add(k):
        y_copy(k).wait_recv()
        total = core_sums[k * 2 + y].astype(jnp.float32) + from_y[k].astype(jnp.float32)
        y_sums[k] = total.astype(jnp.bfloat16)

    def y_send(k):
        y_add(lax.rem(z + k, z_size))
        z_copy(k).start()

    loop(1, z_size, y_send)
    y_add(z)
    total = stream[aligned(me, width), :].astype(jnp.float32) + y_sums[z].astype(jnp.float32)

    def z_add(k, total):
        z_copy(k).wait_recv()
        return total + from_z[k - 1].astype(jnp.float32)

    total = lax.fori_loop(1, z_size, z_add, total)
    layer_out = total.astype(jnp.bfloat16)
    layer_ref[...] = layer_out
    final_stream[aligned(me, width), :] = layer_out
    gather(3, feature_block(final_stream))

    def summed(k):
        core_copy(k).wait_send()

    loop(0, n_expert, summed)
    loop(0, z_size, lambda k: y_copy(k).wait_send())
    loop(1, z_size, lambda k: z_copy(k).wait_send())

    normalise(final_stream, lm_gain_ref)
    loads[3].wait()

    def project(i):
        columns = aligned(i, TILE)
        product = jnp.dot(rows_major[...], vocab[:, columns], preferred_element_type=jnp.float32)
        logits[columns, :] = product.T

    loop(0, logits.shape[0] // TILE, project)
    best = jnp.concatenate(best_of(logits, logits.shape[0] // 8, rows), axis=0)
    candidates[aligned(me, TOPK), :] = best

    def offer(k):
        own = candidates.at[aligned(me, TOPK)]
        return remote(4, k - 1, own, own, device(lax.rem(me + k, n_devices)))

    loop(1, n_devices, lambda k: offer(k).start())
    loop(1, n_devices, lambda k: offer(k).wait_recv())
    best_ref[...] = jnp.concatenate(best_of(candidates, n_devices, rows), axis=0)
    loop(1, n_devices, lambda k: offer(k).wait_send())


def shards(
    hidden_in,
    queries,
    new_keys,
    new_values,
    cache_keys,
    cache_values,
    parents,
    lengths,
    out_proj,
    ffn_gain,
    routes,
    route_weights,
    w_gate,
    w_up,
    w_down,
    lm_gain,
    vocab_weight,
):
    n_head = lax.axis_size("head")
    n_expert = lax.axis_size("expert")
    n_devices = n_expert * n_head
    rows, width = hidden_in.shape
    full_width = width * n_devices
    context = attend(queries, new_keys, new_values, cache_keys, cache_values, parents, lengths)
    in_vmem = pl.BlockSpec(memory_space=pltpu.VMEM)
    in_hbm = pl.BlockSpec(memory_space=pl.ANY)
    half16 = lambda *shape: pltpu.VMEM(shape, jnp.bfloat16)
    layer_t, best_t = pl.pallas_call(
        functools.partial(layer_kernel, n_expert, n_head),
        out_shape=(
            jax.ShapeDtypeStruct((width, rows), jnp.bfloat16),
            jax.ShapeDtypeStruct((TOPK, rows), jnp.float32),
        ),
        in_specs=[in_vmem] * 6 + [in_hbm] * 3 + [in_vmem, in_hbm],
        out_specs=(in_vmem, in_vmem),
        scratch_shapes=[
            half16(*w_gate.shape),
            half16(*w_up.shape),
            half16(*w_down.shape),
            half16(*vocab_weight.shape),
            pltpu.SemaphoreType.DMA((4,)),
            half16(n_head, n_expert * context.shape[0], context.shape[1]),
            half16(full_width, rows),
            half16(full_width, rows),
            half16(rows, full_width),
            half16(rows, w_gate.shape[1]),
            half16(full_width, rows),
            half16(n_expert, width, rows),
            half16(n_expert, width, rows),
            half16(n_expert // 2, width, rows),
            half16(n_expert // 2, width, rows),
            half16(n_expert // 2, width, rows),
            pltpu.VMEM((vocab_weight.shape[1], rows), jnp.float32),
            pltpu.VMEM((n_devices * TOPK, rows), jnp.float32),
            pltpu.SemaphoreType.DMA((5, n_devices - 1)),
            pltpu.SemaphoreType.DMA((5, n_devices - 1)),
        ],
        compiler_params=pltpu.CompilerParams(
            collective_id=0, has_side_effects=True, vmem_limit_bytes=60 * 2**20
        ),
    )(
        context,
        out_proj.T,
        hidden_in.T,
        ffn_gain[None],
        routes.T,
        route_weights.T,
        w_gate,
        w_up,
        w_down,
        lm_gain[None],
        vocab_weight,
    )
    return (layer_t.T, best_t.T)


def solution(mesh):
    placed = (
        P("rep", ("expert", "head")),
        P(("rep", "expert"), "head", None, None),
        P(("rep", "expert"), "head", None),
        P(("rep", "expert"), "head", None),
        P(("rep", "expert"), "head", None, None),
        P(("rep", "expert"), "head", None, None),
        P(("rep", "expert")),
        P(("rep", "expert")),
        P(None, ("expert", "head")),
        P(),
        P("rep", None),
        P("rep", None),
        P(None, ("expert", "head")),
        P(None, ("expert", "head")),
        P(("expert", "head"), None),
        P(),
        P(None, ("expert", "head")),
    )
    return jax.shard_map(
        shards,
        mesh=mesh,
        in_specs=placed,
        out_specs=(P("rep", ("expert", "head")), P("rep", None)),
        check_vma=False,
    )
```

```python
import functools
import math

import jax
import jax.numpy as jnp
from jax import lax
from jax.experimental import pallas as pl
from jax.experimental.pallas import tpu as pltpu
from jax.sharding import PartitionSpec as P

E = 4
BEAM = 8
TOPK = 8


def attend(queries, new_keys, new_values, cache_keys, cache_values, parents, lengths):
    row_count = queries.shape[0]
    beam_base = jnp.arange(row_count, dtype=jnp.int32) // BEAM * BEAM
    source = beam_base + parents
    picked_keys = jnp.take(cache_keys, source, axis=0)
    picked_values = jnp.take(cache_values, source, axis=0)
    factor = 1.0 / math.sqrt(queries.shape[-1])
    scores = (
        jnp.einsum("rgjd,rgtd->rgjt", queries, picked_keys, preferred_element_type=jnp.float32)
        * factor
    )
    fresh_score = (
        jnp.einsum("rgjd,rgd->rgj", queries, new_keys, preferred_element_type=jnp.float32) * factor
    )
    limits = jnp.repeat(lengths, BEAM)
    in_cache = jnp.arange(cache_keys.shape[2], dtype=jnp.int32)[None, :] < limits[:, None]
    scores = jnp.where(in_cache[:, None, None, :], scores, -1e30)
    highest = jnp.maximum(jnp.max(scores, axis=-1), fresh_score)
    expo = jnp.exp(scores - highest[..., None])
    own_term = jnp.exp(fresh_score - highest)
    denominator = jnp.sum(expo, axis=-1) + own_term
    weights = (expo / denominator[..., None]).astype(jnp.bfloat16)
    own_weight = (own_term / denominator).astype(jnp.bfloat16)
    context = jnp.einsum(
        "rgjt,rgtd->rgjd", weights, picked_values, preferred_element_type=jnp.float32
    )
    context = (
        context
        + own_weight.astype(jnp.float32)[..., None] * new_values.astype(jnp.float32)[:, :, None, :]
    )
    return context.astype(jnp.bfloat16).reshape(row_count, -1)


TILE = 256
MESH = pl.DeviceIdType.MESH


def aligned(index, size):
    return pl.ds(pl.multiple_of(index * size, size), size)


def best_of(source, groups, width):
    def insert(group, kept):
        item = source[aligned(group, 8), :]
        result = []
        for level in kept:
            result.append(jnp.maximum(level, item))
            item = jnp.minimum(level, item)
        return tuple(result)

    lowest = jnp.full((8, width), -jnp.inf, jnp.float32)
    kept = list(lax.fori_loop(0, groups, insert, (lowest,) * TOPK))
    lane_class = lax.broadcasted_iota(jnp.int32, (8, width), 0)
    best = []
    for _ in range(TOPK):
        top = jnp.max(kept[0], axis=0, keepdims=True)
        first = jnp.min(jnp.where(kept[0] == top, lane_class, 8), axis=0, keepdims=True)
        taken = lane_class == first
        best.append(top)
        kept = [
            jnp.where(taken, kept[j + 1] if j + 1 < TOPK else lowest, kept[j])
            for j in range(TOPK)
        ]
    return best


def layer_kernel(
    n_expert,
    n_head,
    context_ref,
    proj_ref,
    hidden_ref,
    ffn_gain_ref,
    routes_ref,
    route_weights_ref,
    gate_hbm,
    up_hbm,
    down_hbm,
    lm_gain_ref,
    vocab_hbm,
    layer_ref,
    best_ref,
    gate,
    up,
    down,
    vocab,
    load_sem,
    contexts,
    stream,
    final_stream,
    ffn_squares,
    gate_total,
    up_total,
    lm_squares,
    logit_total,
    hidden,
    partials,
    from_core,
    core_sums,
    from_y,
    y_sums,
    from_z,
    logits,
    candidates,
    send_sem,
    recv_sem,
):
    n_devices = n_expert * n_head
    z_size = n_expert // 2
    e = lax.axis_index("expert")
    h = lax.axis_index("head")
    me = e * n_head + h
    z, y = e // 2, lax.rem(e, 2)
    local_rows = context_ref.shape[0]
    width, rows = hidden_ref.shape
    full_width = width * n_devices
    y_peer = {"expert": z * 2 + 1 - y, "head": h}
    core_peer = {"expert": e, "head": 1 - h}

    loads = [
        pltpu.make_async_copy(source, target, load_sem.at[i])
        for i, (source, target) in enumerate(
            ((gate_hbm, gate), (up_hbm, up), (down_hbm, down), (vocab_hbm, vocab))
        )
    ]
    for load in loads:
        load.start()

    def device(index):
        return {"expert": index // n_head, "head": lax.rem(index, n_head)}

    barrier = pltpu.get_barrier_semaphore()

    def greet(k, carry):
        other = lax.rem(me + k, n_devices)
        pl.semaphore_signal(barrier, inc=1, device_id=device(other), device_id_type=MESH)
        return carry

    lax.fori_loop(1, n_devices, greet, 0)
    pl.semaphore_wait(barrier, n_devices - 1)

    def remote(phase, slot, source, target, device_id):
        return pltpu.make_async_remote_copy(
            src_ref=source,
            dst_ref=target,
            send_sem=send_sem.at[phase, slot],
            recv_sem=recv_sem.at[phase, slot],
            device_id=device_id,
            device_id_type=MESH,
        )

    first_y = z_size - 1
    first_core = 2 * z_size - 1

    def loop(start, stop, step):
        def run(k, carry):
            step(k)
            return carry

        lax.fori_loop(start, stop, run, 0)

    def gather(phase, block, consume=None):
        def move(slot, expert, head, device_id):
            return remote(phase, slot, block(expert, head), block(expert, head), device_id)

        own = block(e, h)

        def to_z(k):
            target = lax.rem(z + k, z_size) * 2 + y
            move(k - 1, e, h, {"expert": target, "head": h}).start()

        loop(1, z_size, to_z)
        move(first_y, e, h, y_peer).start()
        move(first_core, e, h, core_peer).start()

        def step(k):
            @pl.when(jnp.logical_and(k >= 0, k < z_size - 1))
            def _():
                expert = lax.rem(z + z_size - k - 1, z_size) * 2 + y
                move(k, expert, h, y_peer).wait_recv()
                move(first_y + k + 1, expert, h, y_peer).start()
                move(first_core + k + 1, expert, h, core_peer).start()

            @pl.when(jnp.logical_and(k >= 0, k < z_size))
            def _():
                expert = lax.rem(z + z_size - k, z_size) * 2 + 1 - y
                move(first_y + k, expert, h, y_peer).wait_recv()
                move(first_core + z_size + k, expert, h, core_peer).start()

            @pl.when(k >= 1)
            def _():
                move(first_core + k - 1, e, 1 - h, core_peer).wait_recv()
                move(first_core + z_size + k - 1, e, 1 - h, core_peer).wait_recv()
                if consume is not None:
                    consume(lax.rem(z + z_size - k + 1, z_size))

        loop(0, z_size + 1, step)

        def sent(k):
            move(k, e, h, core_peer).wait_send()

        loop(0, n_devices - 1, sent)

    def context_block(expert, head):
        return contexts.at[head, aligned(expert, local_rows)]

    def feature_block(buffer):
        return lambda expert, head: buffer.at[aligned(expert * n_head + head, width)]

    contexts[h, aligned(e, local_rows), :] = context_ref[...]
    gather(0, context_block)
    half = context_ref.shape[1]
    attention = hidden_ref[...].astype(jnp.float32)
    for head in range(n_head):
        attention += lax.dot_general(
            proj_ref[:, head * half : (head + 1) * half],
            contexts[head],
            (((1,), (1,)), ((), ())),
            preferred_element_type=jnp.float32,
        )
    residual = attention.astype(jnp.bfloat16)
    stream[aligned(me, width), :] = residual
    group = n_head * 2 * width

    def clear(*totals):
        for total in totals:
            total[...] = jnp.zeros_like(total)

    def multiply(source, gain_ref, squares, pairs):
        def consume(number):
            features = aligned(number, group)
            block = source[features, :].astype(jnp.float32).T
            squares[...] += jnp.sum(block * block, axis=1, keepdims=True)
            block = (block * gain_ref[number]).astype(jnp.bfloat16)

            def tile(i):
                columns = aligned(i, TILE)
                for weight, total in pairs:
                    total[:, columns] += jnp.dot(
                        block, weight[features, columns], preferred_element_type=jnp.float32
                    )

            loop(0, pairs[0][0].shape[1] // TILE, tile)

        return consume

    clear(ffn_squares, gate_total, up_total)
    loads[0].wait()
    loads[1].wait()
    gather(
        1,
        feature_block(stream),
        multiply(stream, ffn_gain_ref, ffn_squares, ((gate, gate_total), (up, up_total))),
    )

    ffn_scale = lax.rsqrt(ffn_squares[...] / full_width + 1e-05)

    def widen(i):
        columns = aligned(i, TILE)
        gate_proj = gate_total[:, columns] * ffn_scale
        up_proj = up_total[:, columns] * ffn_scale
        active = gate_proj / (1.0 + jnp.exp(-gate_proj)) * up_proj
        hidden[:, columns] = active.astype(jnp.bfloat16)

    loop(0, hidden.shape[1] // TILE, widen)
    loads[2].wait()
    expert_here = me // (n_devices // E)
    share = jnp.sum(
        jnp.where(routes_ref[...] == expert_here, route_weights_ref[...], 0.0),
        axis=0,
        keepdims=True,
    )

    def narrow(i):
        columns = aligned(i, TILE)
        product = jnp.dot(hidden[...], down[:, columns], preferred_element_type=jnp.float32)
        partials[columns, :] = (product.T * share).astype(jnp.bfloat16)

    mine = feature_block(partials)

    def core_copy(expert):
        return remote(
            2, first_core + expert, mine(expert, 1 - h), from_core.at[expert], core_peer
        )

    def y_copy(k):
        return remote(2, first_y + k, core_sums.at[k * 2 + 1 - y], from_y.at[k], y_peer)

    def z_copy(k):
        target = lax.rem(z + k, z_size)
        return remote(
            2,
            k - 1,
            y_sums.at[target],
            from_z.at[k - 1],
            {"expert": target * 2 + y, "head": h},
        )

    def core_add(expert):
        core_copy(expert).wait_recv()
        own = partials[aligned(expert * n_head + h, width), :].astype(jnp.float32)
        core_sums[expert] = (own + from_core[expert].astype(jnp.float32)).astype(jnp.bfloat16)

    def y_add(k):
        y_copy(k).wait_recv()
        total = core_sums[k * 2 + y].astype(jnp.float32) + from_y[k].astype(jnp.float32)
        y_sums[k] = total.astype(jnp.bfloat16)

    whole_tiles = group // TILE if group % TILE == 0 else 0
    if not whole_tiles:
        loop(0, full_width // TILE, narrow)

    def scatter_step(k):
        @pl.when(k <= z_size)
        def _():
            target = lax.rem(z + k, z_size)
            if whole_tiles:
                for part in range(whole_tiles):
                    narrow(target * whole_tiles + part)
            core_copy(target * 2 + 1 - y).start()
            core_copy(target * 2 + y).start()

        @pl.when(jnp.logical_and(k >= 2, k <= z_size + 1))
        def _():
            target = lax.rem(z + k - 1, z_size)
            core_add(target * 2 + 1 - y)
            y_copy(target).start()
            core_add(target * 2 + y)

        @pl.when(k >= 3)
        def _():
            y_add(lax.rem(z + k - 2, z_size))

            @pl.when(k - 2 < z_size)
            def _():
                z_copy(k - 2).start()

    loop(1, z_size + 3, scatter_step)
    total = stream[aligned(me, width), :].astype(jnp.float32) + y_sums[z].astype(jnp.float32)

    def z_add(k, total):
        z_copy(k).wait_recv()
        return total + from_z[k - 1].astype(jnp.float32)

    total = lax.fori_loop(1, z_size, z_add, total)
    layer_out = total.astype(jnp.bfloat16)
    layer_ref[...] = layer_out
    final_stream[aligned(me, width), :] = layer_out
    clear(lm_squares, logit_total)
    loads[3].wait()
    gather(
        3,
        feature_block(final_stream),
        multiply(final_stream, lm_gain_ref, lm_squares, ((vocab, logit_total),)),
    )

    def summed(k):
        core_copy(k).wait_send()

    loop(0, n_expert, summed)
    loop(0, z_size, lambda k: y_copy(k).wait_send())
    loop(1, z_size, lambda k: z_copy(k).wait_send())

    lm_scale = lax.rsqrt(lm_squares[...] / full_width + 1e-05)

    def project(i):
        columns = aligned(i, TILE)
        logits[columns, :] = (logit_total[:, columns] * lm_scale).T

    loop(0, logits.shape[0] // TILE, project)
    best = jnp.concatenate(best_of(logits, logits.shape[0] // 8, rows), axis=0)
    candidates[aligned(me, TOPK), :] = best

    def offer(k):
        own = candidates.at[aligned(me, TOPK)]
        return remote(4, k - 1, own, own, device(lax.rem(me + k, n_devices)))

    loop(1, n_devices, lambda k: offer(k).start())
    loop(1, n_devices, lambda k: offer(k).wait_recv())
    best_ref[...] = jnp.concatenate(best_of(candidates, n_devices, rows), axis=0)
    loop(1, n_devices, lambda k: offer(k).wait_send())


def shards(
    hidden_in,
    queries,
    new_keys,
    new_values,
    cache_keys,
    cache_values,
    parents,
    lengths,
    out_proj,
    ffn_gain,
    routes,
    route_weights,
    w_gate,
    w_up,
    w_down,
    lm_gain,
    vocab_weight,
):
    n_head = lax.axis_size("head")
    n_expert = lax.axis_size("expert")
    n_devices = n_expert * n_head
    rows, width = hidden_in.shape
    full_width = width * n_devices
    context = attend(queries, new_keys, new_values, cache_keys, cache_values, parents, lengths)
    in_vmem = pl.BlockSpec(memory_space=pltpu.VMEM)
    in_hbm = pl.BlockSpec(memory_space=pl.ANY)
    half16 = lambda *shape: pltpu.VMEM(shape, jnp.bfloat16)
    layer_t, best_t = pl.pallas_call(
        functools.partial(layer_kernel, n_expert, n_head),
        out_shape=(
            jax.ShapeDtypeStruct((width, rows), jnp.bfloat16),
            jax.ShapeDtypeStruct((TOPK, rows), jnp.float32),
        ),
        in_specs=[in_vmem] * 6 + [in_hbm] * 3 + [in_vmem, in_hbm],
        out_specs=(in_vmem, in_vmem),
        scratch_shapes=[
            half16(*w_gate.shape),
            half16(*w_up.shape),
            half16(*w_down.shape),
            half16(*vocab_weight.shape),
            pltpu.SemaphoreType.DMA((4,)),
            half16(n_head, n_expert * context.shape[0], context.shape[1]),
            half16(full_width, rows),
            half16(full_width, rows),
            pltpu.VMEM((rows, 1), jnp.float32),
            pltpu.VMEM((rows, w_gate.shape[1]), jnp.float32),
            pltpu.VMEM((rows, w_gate.shape[1]), jnp.float32),
            pltpu.VMEM((rows, 1), jnp.float32),
            pltpu.VMEM((rows, vocab_weight.shape[1]), jnp.float32),
            half16(rows, w_gate.shape[1]),
            half16(full_width, rows),
            half16(n_expert, width, rows),
            half16(n_expert, width, rows),
            half16(n_expert // 2, width, rows),
            half16(n_expert // 2, width, rows),
            half16(n_expert // 2, width, rows),
            pltpu.VMEM((vocab_weight.shape[1], rows), jnp.float32),
            pltpu.VMEM((n_devices * TOPK, rows), jnp.float32),
            pltpu.SemaphoreType.DMA((5, n_devices - 1)),
            pltpu.SemaphoreType.DMA((5, n_devices - 1)),
        ],
        compiler_params=pltpu.CompilerParams(
            collective_id=0, has_side_effects=True, vmem_limit_bytes=60 * 2**20
        ),
    )(
        context,
        out_proj.T,
        hidden_in.T,
        ffn_gain.reshape(n_expert // 2, 1, -1),
        routes.T,
        route_weights.T,
        w_gate,
        w_up,
        w_down,
        lm_gain.reshape(n_expert // 2, 1, -1),
        vocab_weight,
    )
    return (layer_t.T, best_t.T)


def solution(mesh):
    placed = (
        P("rep", ("expert", "head")),
        P(("rep", "expert"), "head", None, None),
        P(("rep", "expert"), "head", None),
        P(("rep", "expert"), "head", None),
        P(("rep", "expert"), "head", None, None),
        P(("rep", "expert"), "head", None, None),
        P(("rep", "expert")),
        P(("rep", "expert")),
        P(None, ("expert", "head")),
        P(),
        P("rep", None),
        P("rep", None),
        P(None, ("expert", "head")),
        P(None, ("expert", "head")),
        P(("expert", "head"), None),
        P(),
        P(None, ("expert", "head")),
    )
    return jax.shard_map(
        shards,
        mesh=mesh,
        in_specs=placed,
        out_specs=(P("rep", ("expert", "head")), P("rep", None)),
        check_vma=False,
    )
```

```python
import functools
import math

import jax
import jax.numpy as jnp
from jax import lax
from jax.experimental import pallas as pl
from jax.experimental.pallas import tpu as pltpu
from jax.sharding import PartitionSpec as P

E = 4
BEAM = 8
TOPK = 8


def attend(queries, new_keys, new_values, cache_keys, cache_values, parents, lengths):
    row_count = queries.shape[0]
    beam_base = jnp.arange(row_count, dtype=jnp.int32) // BEAM * BEAM
    source = beam_base + parents
    picked_keys = jnp.take(cache_keys, source, axis=0)
    picked_values = jnp.take(cache_values, source, axis=0)
    factor = 1.0 / math.sqrt(queries.shape[-1])
    scores = (
        jnp.einsum("rgjd,rgtd->rgjt", queries, picked_keys, preferred_element_type=jnp.float32)
        * factor
    )
    fresh_score = (
        jnp.einsum("rgjd,rgd->rgj", queries, new_keys, preferred_element_type=jnp.float32) * factor
    )
    limits = jnp.repeat(lengths, BEAM)
    in_cache = jnp.arange(cache_keys.shape[2], dtype=jnp.int32)[None, :] < limits[:, None]
    scores = jnp.where(in_cache[:, None, None, :], scores, -1e30)
    highest = jnp.maximum(jnp.max(scores, axis=-1), fresh_score)
    expo = jnp.exp(scores - highest[..., None])
    own_term = jnp.exp(fresh_score - highest)
    denominator = jnp.sum(expo, axis=-1) + own_term
    weights = (expo / denominator[..., None]).astype(jnp.bfloat16)
    own_weight = (own_term / denominator).astype(jnp.bfloat16)
    context = jnp.einsum(
        "rgjt,rgtd->rgjd", weights, picked_values, preferred_element_type=jnp.float32
    )
    context = (
        context
        + own_weight.astype(jnp.float32)[..., None] * new_values.astype(jnp.float32)[:, :, None, :]
    )
    return context.astype(jnp.bfloat16).reshape(row_count, -1)


TILE = 256
MESH = pl.DeviceIdType.MESH


def aligned(index, size):
    if isinstance(index, int):
        return pl.ds(index * size, size)
    return pl.ds(pl.multiple_of(index * size, size), size)


def best_of(source, groups, width):
    def insert(group, kept):
        item = source[aligned(group, 8), :]
        result = []
        for level in kept:
            result.append(jnp.maximum(level, item))
            item = jnp.minimum(level, item)
        return tuple(result)

    lowest = jnp.full((8, width), -jnp.inf, jnp.float32)
    kept = list(lax.fori_loop(0, groups, insert, (lowest,) * TOPK, unroll=8))
    lane_class = lax.broadcasted_iota(jnp.int32, (8, width), 0)
    best = []
    for _ in range(TOPK):
        top = jnp.max(kept[0], axis=0, keepdims=True)
        first = jnp.min(jnp.where(kept[0] == top, lane_class, 8), axis=0, keepdims=True)
        taken = lane_class == first
        best.append(top)
        kept = [
            jnp.where(taken, kept[j + 1] if j + 1 < TOPK else lowest, kept[j])
            for j in range(TOPK)
        ]
    return best


def layer_kernel(
    n_expert,
    n_head,
    context_ref,
    proj_ref,
    hidden_ref,
    ffn_gain_ref,
    routes_ref,
    route_weights_ref,
    gate_hbm,
    up_hbm,
    down_hbm,
    lm_gain_ref,
    vocab_hbm,
    layer_ref,
    best_ref,
    gate,
    up,
    down,
    vocab,
    load_sem,
    contexts,
    stream,
    final_stream,
    ffn_squares,
    gate_total,
    up_total,
    lm_squares,
    logit_total,
    hidden,
    partials,
    from_core,
    core_sums,
    from_y,
    y_sums,
    from_z,
    logits,
    candidates,
    send_sem,
    recv_sem,
):
    n_devices = n_expert * n_head
    z_size = n_expert // 2
    e = lax.axis_index("expert")
    h = lax.axis_index("head")
    me = e * n_head + h
    z, y = e // 2, lax.rem(e, 2)
    local_rows = context_ref.shape[0]
    width, rows = hidden_ref.shape
    full_width = width * n_devices
    y_peer = {"expert": z * 2 + 1 - y, "head": h}
    core_peer = {"expert": e, "head": 1 - h}

    loads = [
        pltpu.make_async_copy(source, target, load_sem.at[i])
        for i, (source, target) in enumerate(
            ((gate_hbm, gate), (up_hbm, up), (down_hbm, down), (vocab_hbm, vocab))
        )
    ]
    for load in loads:
        load.start()

    def device(index):
        return {"expert": index // n_head, "head": lax.rem(index, n_head)}

    barrier = pltpu.get_barrier_semaphore()

    def greet(k, carry):
        other = lax.rem(me + k, n_devices)
        pl.semaphore_signal(barrier, inc=1, device_id=device(other), device_id_type=MESH)
        return carry

    lax.fori_loop(1, n_devices, greet, 0)
    pl.semaphore_wait(barrier, n_devices - 1)

    def remote(phase, slot, source, target, device_id):
        return pltpu.make_async_remote_copy(
            src_ref=source,
            dst_ref=target,
            send_sem=send_sem.at[phase, slot],
            recv_sem=recv_sem.at[phase, slot],
            device_id=device_id,
            device_id_type=MESH,
        )

    first_y = z_size - 1
    first_core = 2 * z_size - 1

    def loop(start, stop, step):
        def run(k, carry):
            step(k)
            return carry

        lax.fori_loop(start, stop, run, 0)

    def gather(phase, block, consume=None):
        def move(slot, expert, head, device_id):
            return remote(phase, slot, block(expert, head), block(expert, head), device_id)

        own = block(e, h)

        def to_z(k):
            target = lax.rem(z + k, z_size) * 2 + y
            move(k - 1, e, h, {"expert": target, "head": h}).start()

        loop(1, z_size, to_z)
        move(first_y, e, h, y_peer).start()
        move(first_core, e, h, core_peer).start()

        def step(k):
            @pl.when(jnp.logical_and(k >= 0, k < z_size - 1))
            def _():
                expert = lax.rem(z + z_size - k - 1, z_size) * 2 + y
                move(k, expert, h, y_peer).wait_recv()
                move(first_y + k + 1, expert, h, y_peer).start()
                move(first_core + k + 1, expert, h, core_peer).start()

            @pl.when(jnp.logical_and(k >= 0, k < z_size))
            def _():
                expert = lax.rem(z + z_size - k, z_size) * 2 + 1 - y
                move(first_y + k, expert, h, y_peer).wait_recv()
                move(first_core + z_size + k, expert, h, core_peer).start()

            @pl.when(k >= 1)
            def _():
                move(first_core + k - 1, e, 1 - h, core_peer).wait_recv()
                move(first_core + z_size + k - 1, e, 1 - h, core_peer).wait_recv()
                if consume is not None:
                    consume(lax.rem(z + z_size - k + 1, z_size))

        loop(0, z_size + 1, step)

        def sent(k):
            move(k, e, h, core_peer).wait_send()

        loop(0, n_devices - 1, sent)

    def context_block(expert, head):
        return contexts.at[head, aligned(expert, local_rows)]

    def feature_block(buffer):
        return lambda expert, head: buffer.at[aligned(expert * n_head + head, width)]

    contexts[h, aligned(e, local_rows), :] = context_ref[...]
    gather(0, context_block)
    half = context_ref.shape[1]
    attention = hidden_ref[...].astype(jnp.float32)
    for head in range(n_head):
        attention += lax.dot_general(
            proj_ref[:, head * half : (head + 1) * half],
            contexts[head],
            (((1,), (1,)), ((), ())),
            preferred_element_type=jnp.float32,
        )
    residual = attention.astype(jnp.bfloat16)
    stream[aligned(me, width), :] = residual
    group = n_head * 2 * width

    def clear(*totals):
        for total in totals:
            total[...] = jnp.zeros_like(total)

    def multiply(source, gain_ref, squares, pairs):
        def consume(number):
            features = aligned(number, group)
            block = source[features, :].astype(jnp.float32).T
            squares[...] += jnp.sum(block * block, axis=1, keepdims=True)
            block = (block * gain_ref[number]).astype(jnp.bfloat16)

            for weight, total in pairs:
                total[...] += jnp.dot(block, weight[features, :], preferred_element_type=jnp.float32)

        return consume

    clear(ffn_squares, gate_total, up_total)
    loads[0].wait()
    loads[1].wait()
    gather(
        1,
        feature_block(stream),
        multiply(stream, ffn_gain_ref, ffn_squares, ((gate, gate_total), (up, up_total))),
    )

    ffn_scale = lax.rsqrt(ffn_squares[...] / full_width + 1e-05)

    def widen(i):
        columns = aligned(i, TILE)
        gate_proj = gate_total[:, columns] * ffn_scale
        up_proj = up_total[:, columns] * ffn_scale
        active = gate_proj / (1.0 + jnp.exp(-gate_proj)) * up_proj
        hidden[:, columns] = active.astype(jnp.bfloat16)

    for i in range(hidden.shape[1] // TILE):
        widen(i)
    loads[2].wait()
    expert_here = me // (n_devices // E)
    share = jnp.sum(
        jnp.where(routes_ref[...] == expert_here, route_weights_ref[...], 0.0),
        axis=0,
        keepdims=True,
    )

    def narrow(i):
        columns = aligned(i, TILE)
        product = jnp.dot(hidden[...], down[:, columns], preferred_element_type=jnp.float32)
        partials[columns, :] = (product.T * share).astype(jnp.bfloat16)

    mine = feature_block(partials)

    def core_copy(expert):
        return remote(
            2, first_core + expert, mine(expert, 1 - h), from_core.at[expert], core_peer
        )

    def y_copy(k):
        return remote(2, first_y + k, core_sums.at[k * 2 + 1 - y], from_y.at[k], y_peer)

    def z_copy(k):
        target = lax.rem(z + k, z_size)
        return remote(
            2,
            k - 1,
            y_sums.at[target],
            from_z.at[k - 1],
            {"expert": target * 2 + y, "head": h},
        )

    def core_add(expert):
        core_copy(expert).wait_recv()
        own = partials[aligned(expert * n_head + h, width), :].astype(jnp.float32)
        core_sums[expert] = (own + from_core[expert].astype(jnp.float32)).astype(jnp.bfloat16)

    def y_add(k):
        y_copy(k).wait_recv()
        total = core_sums[k * 2 + y].astype(jnp.float32) + from_y[k].astype(jnp.float32)
        y_sums[k] = total.astype(jnp.bfloat16)

    whole_tiles = group // TILE if group % TILE == 0 else 0
    if not whole_tiles:
        loop(0, full_width // TILE, narrow)

    def scatter_step(k):
        @pl.when(k <= z_size)
        def _():
            target = lax.rem(z + k, z_size)
            if whole_tiles:
                for part in range(whole_tiles):
                    narrow(target * whole_tiles + part)
            core_copy(target * 2 + 1 - y).start()
            core_copy(target * 2 + y).start()

        @pl.when(jnp.logical_and(k >= 2, k <= z_size + 1))
        def _():
            target = lax.rem(z + k - 1, z_size)
            core_add(target * 2 + 1 - y)
            y_copy(target).start()
            core_add(target * 2 + y)

        @pl.when(k >= 3)
        def _():
            y_add(lax.rem(z + k - 2, z_size))

            @pl.when(k - 2 < z_size)
            def _():
                z_copy(k - 2).start()

    loop(1, z_size + 3, scatter_step)
    total = stream[aligned(me, width), :].astype(jnp.float32) + y_sums[z].astype(jnp.float32)

    def z_add(k, total):
        z_copy(k).wait_recv()
        return total + from_z[k - 1].astype(jnp.float32)

    total = lax.fori_loop(1, z_size, z_add, total)
    layer_out = total.astype(jnp.bfloat16)
    layer_ref[...] = layer_out
    final_stream[aligned(me, width), :] = layer_out
    clear(lm_squares, logit_total)
    loads[3].wait()
    gather(
        3,
        feature_block(final_stream),
        multiply(final_stream, lm_gain_ref, lm_squares, ((vocab, logit_total),)),
    )

    def summed(k):
        core_copy(k).wait_send()

    loop(0, n_expert, summed)
    loop(0, z_size, lambda k: y_copy(k).wait_send())
    loop(1, z_size, lambda k: z_copy(k).wait_send())

    lm_scale = lax.rsqrt(lm_squares[...] / full_width + 1e-05)

    def project(i):
        columns = aligned(i, TILE)
        logits[columns, :] = (logit_total[:, columns] * lm_scale).T

    for i in range(logits.shape[0] // TILE):
        project(i)
    best = jnp.concatenate(best_of(logits, logits.shape[0] // 8, rows), axis=0)
    candidates[aligned(me, TOPK), :] = best

    def offer(k):
        own = candidates.at[aligned(me, TOPK)]
        return remote(4, k - 1, own, own, device(lax.rem(me + k, n_devices)))

    loop(1, n_devices, lambda k: offer(k).start())
    loop(1, n_devices, lambda k: offer(k).wait_recv())
    best_ref[...] = jnp.concatenate(best_of(candidates, n_devices, rows), axis=0)
    loop(1, n_devices, lambda k: offer(k).wait_send())


def shards(
    hidden_in,
    queries,
    new_keys,
    new_values,
    cache_keys,
    cache_values,
    parents,
    lengths,
    out_proj,
    ffn_gain,
    routes,
    route_weights,
    w_gate,
    w_up,
    w_down,
    lm_gain,
    vocab_weight,
):
    n_head = lax.axis_size("head")
    n_expert = lax.axis_size("expert")
    n_devices = n_expert * n_head
    rows, width = hidden_in.shape
    full_width = width * n_devices
    context = attend(queries, new_keys, new_values, cache_keys, cache_values, parents, lengths)
    in_vmem = pl.BlockSpec(memory_space=pltpu.VMEM)
    in_hbm = pl.BlockSpec(memory_space=pl.ANY)
    half16 = lambda *shape: pltpu.VMEM(shape, jnp.bfloat16)
    layer_t, best_t = pl.pallas_call(
        functools.partial(layer_kernel, n_expert, n_head),
        out_shape=(
            jax.ShapeDtypeStruct((width, rows), jnp.bfloat16),
            jax.ShapeDtypeStruct((TOPK, rows), jnp.float32),
        ),
        in_specs=[in_vmem] * 6 + [in_hbm] * 3 + [in_vmem, in_hbm],
        out_specs=(in_vmem, in_vmem),
        scratch_shapes=[
            half16(*w_gate.shape),
            half16(*w_up.shape),
            half16(*w_down.shape),
            half16(*vocab_weight.shape),
            pltpu.SemaphoreType.DMA((4,)),
            half16(n_head, n_expert * context.shape[0], context.shape[1]),
            half16(full_width, rows),
            half16(full_width, rows),
            pltpu.VMEM((rows, 1), jnp.float32),
            pltpu.VMEM((rows, w_gate.shape[1]), jnp.float32),
            pltpu.VMEM((rows, w_gate.shape[1]), jnp.float32),
            pltpu.VMEM((rows, 1), jnp.float32),
            pltpu.VMEM((rows, vocab_weight.shape[1]), jnp.float32),
            half16(rows, w_gate.shape[1]),
            half16(full_width, rows),
            half16(n_expert, width, rows),
            half16(n_expert, width, rows),
            half16(n_expert // 2, width, rows),
            half16(n_expert // 2, width, rows),
            half16(n_expert // 2, width, rows),
            pltpu.VMEM((vocab_weight.shape[1], rows), jnp.float32),
            pltpu.VMEM((n_devices * TOPK, rows), jnp.float32),
            pltpu.SemaphoreType.DMA((5, n_devices - 1)),
            pltpu.SemaphoreType.DMA((5, n_devices - 1)),
        ],
        compiler_params=pltpu.CompilerParams(
            collective_id=0, has_side_effects=True, vmem_limit_bytes=60 * 2**20
        ),
    )(
        context,
        out_proj.T,
        hidden_in.T,
        ffn_gain.reshape(n_expert // 2, 1, -1),
        routes.T,
        route_weights.T,
        w_gate,
        w_up,
        w_down,
        lm_gain.reshape(n_expert // 2, 1, -1),
        vocab_weight,
    )
    return (layer_t.T, best_t.T)


def solution(mesh):
    placed = (
        P("rep", ("expert", "head")),
        P(("rep", "expert"), "head", None, None),
        P(("rep", "expert"), "head", None),
        P(("rep", "expert"), "head", None),
        P(("rep", "expert"), "head", None, None),
        P(("rep", "expert"), "head", None, None),
        P(("rep", "expert")),
        P(("rep", "expert")),
        P(None, ("expert", "head")),
        P(),
        P("rep", None),
        P("rep", None),
        P(None, ("expert", "head")),
        P(None, ("expert", "head")),
        P(("expert", "head"), None),
        P(),
        P(None, ("expert", "head")),
    )
    return jax.shard_map(
        shards,
        mesh=mesh,
        in_specs=placed,
        out_specs=(P("rep", ("expert", "head")), P("rep", None)),
        check_vma=False,
    )
```

```python
import functools
import math

import jax
import jax.numpy as jnp
from jax import lax
from jax.experimental import pallas as pl
from jax.experimental.pallas import tpu as pltpu
from jax.sharding import PartitionSpec as P

E = 4
BEAM = 8
TOPK = 8


def attend(queries, new_keys, new_values, cache_keys, cache_values, parents, lengths):
    row_count = queries.shape[0]
    beam_base = jnp.arange(row_count, dtype=jnp.int32) // BEAM * BEAM
    source = beam_base + parents
    picked_keys = jnp.take(cache_keys, source, axis=0)
    picked_values = jnp.take(cache_values, source, axis=0)
    factor = 1.0 / math.sqrt(queries.shape[-1])
    scores = (
        jnp.einsum("rgjd,rgtd->rgjt", queries, picked_keys, preferred_element_type=jnp.float32)
        * factor
    )
    fresh_score = (
        jnp.einsum("rgjd,rgd->rgj", queries, new_keys, preferred_element_type=jnp.float32) * factor
    )
    limits = jnp.repeat(lengths, BEAM)
    in_cache = jnp.arange(cache_keys.shape[2], dtype=jnp.int32)[None, :] < limits[:, None]
    scores = jnp.where(in_cache[:, None, None, :], scores, -1e30)
    highest = jnp.maximum(jnp.max(scores, axis=-1), fresh_score)
    expo = jnp.exp(scores - highest[..., None])
    own_term = jnp.exp(fresh_score - highest)
    denominator = jnp.sum(expo, axis=-1) + own_term
    weights = (expo / denominator[..., None]).astype(jnp.bfloat16)
    own_weight = (own_term / denominator).astype(jnp.bfloat16)
    context = jnp.einsum(
        "rgjt,rgtd->rgjd", weights, picked_values, preferred_element_type=jnp.float32
    )
    context = (
        context
        + own_weight.astype(jnp.float32)[..., None] * new_values.astype(jnp.float32)[:, :, None, :]
    )
    return context.astype(jnp.bfloat16).reshape(row_count, -1)


TILE = 256
MESH = pl.DeviceIdType.MESH


def aligned(index, size):
    if isinstance(index, int):
        return pl.ds(index * size, size)
    return pl.ds(pl.multiple_of(index * size, size), size)


def best_of(source, groups, width):
    def insert(group, kept):
        item = source[aligned(group, 8), :]
        result = []
        for level in kept:
            result.append(jnp.maximum(level, item))
            item = jnp.minimum(level, item)
        return tuple(result)

    lowest = jnp.full((8, width), -jnp.inf, jnp.float32)
    kept = list(lax.fori_loop(0, groups, insert, (lowest,) * TOPK, unroll=8))
    lane_class = lax.broadcasted_iota(jnp.int32, (8, width), 0)
    best = []
    for _ in range(TOPK):
        top = jnp.max(kept[0], axis=0, keepdims=True)
        first = jnp.min(jnp.where(kept[0] == top, lane_class, 8), axis=0, keepdims=True)
        taken = lane_class == first
        best.append(top)
        kept = [
            jnp.where(taken, kept[j + 1] if j + 1 < TOPK else lowest, kept[j])
            for j in range(TOPK)
        ]
    return best


def layer_kernel(
    n_expert,
    n_head,
    context_ref,
    proj_ref,
    hidden_ref,
    ffn_gain_ref,
    routes_ref,
    route_weights_ref,
    gate_hbm,
    up_hbm,
    down_hbm,
    lm_gain_ref,
    vocab_hbm,
    layer_ref,
    best_ref,
    gate,
    up,
    down,
    vocab,
    load_sem,
    contexts,
    stream,
    final_stream,
    ffn_squares,
    gate_total,
    up_total,
    lm_squares,
    logit_total,
    hidden,
    partials,
    from_core,
    core_sums,
    from_y,
    y_sums,
    from_z,
    logits,
    candidates,
    send_sem,
    recv_sem,
):
    n_devices = n_expert * n_head
    z_size = n_expert // 2
    e = lax.axis_index("expert")
    h = lax.axis_index("head")
    me = e * n_head + h
    z, y = e // 2, lax.rem(e, 2)
    local_rows = context_ref.shape[0]
    width, rows = hidden_ref.shape
    full_width = width * n_devices
    y_peer = {"expert": z * 2 + 1 - y, "head": h}
    core_peer = {"expert": e, "head": 1 - h}

    loads = [
        pltpu.make_async_copy(source, target, load_sem.at[i])
        for i, (source, target) in enumerate(
            ((gate_hbm, gate), (up_hbm, up), (down_hbm, down), (vocab_hbm, vocab))
        )
    ]
    for load in loads:
        load.start()

    def device(index):
        return {"expert": index // n_head, "head": lax.rem(index, n_head)}

    barrier = pltpu.get_barrier_semaphore()

    def greet(k, carry):
        other = lax.rem(me + k, n_devices)
        pl.semaphore_signal(barrier, inc=1, device_id=device(other), device_id_type=MESH)
        return carry

    lax.fori_loop(1, n_devices, greet, 0)
    pl.semaphore_wait(barrier, n_devices - 1)

    def remote(phase, slot, source, target, device_id):
        return pltpu.make_async_remote_copy(
            src_ref=source,
            dst_ref=target,
            send_sem=send_sem.at[phase, slot],
            recv_sem=recv_sem.at[phase, slot],
            device_id=device_id,
            device_id_type=MESH,
        )

    first_y = z_size - 1
    first_core = 2 * z_size - 1

    def loop(start, stop, step):
        def run(k, carry):
            step(k)
            return carry

        lax.fori_loop(start, stop, run, 0)

    def gather(phase, block, consume=None):
        def move(slot, expert, head, device_id):
            return remote(phase, slot, block(expert, head), block(expert, head), device_id)

        own = block(e, h)

        def to_z(k):
            target = lax.rem(z + k, z_size) * 2 + y
            move(k - 1, e, h, {"expert": target, "head": h}).start()

        loop(1, z_size, to_z)
        move(first_y, e, h, y_peer).start()
        move(first_core, e, h, core_peer).start()

        def step(k):
            @pl.when(jnp.logical_and(k >= 0, k < z_size - 1))
            def _():
                expert = lax.rem(z + z_size - k - 1, z_size) * 2 + y
                move(k, expert, h, y_peer).wait_recv()
                move(first_y + k + 1, expert, h, y_peer).start()
                move(first_core + k + 1, expert, h, core_peer).start()

            @pl.when(jnp.logical_and(k >= 0, k < z_size))
            def _():
                expert = lax.rem(z + z_size - k, z_size) * 2 + 1 - y
                move(first_y + k, expert, h, y_peer).wait_recv()
                move(first_core + z_size + k, expert, h, core_peer).start()

            @pl.when(k >= 1)
            def _():
                move(first_core + k - 1, e, 1 - h, core_peer).wait_recv()
                move(first_core + z_size + k - 1, e, 1 - h, core_peer).wait_recv()
                if consume is not None:
                    consume(lax.rem(z + z_size - k + 1, z_size))

        loop(0, z_size + 1, step)

        def sent(k):
            move(k, e, h, core_peer).wait_send()

        loop(0, n_devices - 1, sent)

    def context_block(expert, head):
        return contexts.at[head, aligned(expert, local_rows)]

    def feature_block(buffer):
        return lambda expert, head: buffer.at[aligned(expert * n_head + head, width)]

    contexts[h, aligned(e, local_rows), :] = context_ref[...]
    gather(0, context_block)
    half = context_ref.shape[1]
    attention = hidden_ref[...].astype(jnp.float32)
    for head in range(n_head):
        attention += lax.dot_general(
            proj_ref[:, head * half : (head + 1) * half],
            contexts[head],
            (((1,), (1,)), ((), ())),
            preferred_element_type=jnp.float32,
        )
    residual = attention.astype(jnp.bfloat16)
    stream[aligned(me, width), :] = residual
    group = n_head * 2 * width

    def clear(*totals):
        for total in totals:
            total[...] = jnp.zeros_like(total)

    def multiply(source, gain_ref, squares, pairs):
        def consume(number):
            features = aligned(number, group)
            block = source[features, :].astype(jnp.float32).T
            squares[...] += jnp.sum(block * block, axis=1, keepdims=True)
            block = (block * gain_ref[number]).astype(jnp.bfloat16)

            for weight, total in pairs:
                total[...] += jnp.dot(block, weight[features, :], preferred_element_type=jnp.float32)

        return consume

    clear(ffn_squares, gate_total, up_total)
    loads[0].wait()
    loads[1].wait()
    gather(
        1,
        feature_block(stream),
        multiply(stream, ffn_gain_ref, ffn_squares, ((gate, gate_total), (up, up_total))),
    )

    ffn_scale = lax.rsqrt(ffn_squares[...] / full_width + 1e-05)

    def widen(i):
        columns = aligned(i, TILE)
        gate_proj = gate_total[:, columns] * ffn_scale
        up_proj = up_total[:, columns] * ffn_scale
        active = gate_proj / (1.0 + jnp.exp(-gate_proj)) * up_proj
        hidden[:, columns] = active.astype(jnp.bfloat16)

    for i in range(hidden.shape[1] // TILE):
        widen(i)
    loads[2].wait()
    expert_here = me // (n_devices // E)
    share = jnp.sum(
        jnp.where(routes_ref[...] == expert_here, route_weights_ref[...], 0.0),
        axis=0,
        keepdims=True,
    )

    def narrow(i, size=TILE):
        columns = aligned(i, size)
        product = jnp.dot(hidden[...], down[:, columns], preferred_element_type=jnp.float32)
        partials[columns, :] = (product.T * share).astype(jnp.bfloat16)

    mine = feature_block(partials)

    def core_copy(expert):
        return remote(
            2, first_core + expert, mine(expert, 1 - h), from_core.at[expert], core_peer
        )

    def y_copy(k):
        return remote(2, first_y + k, core_sums.at[k * 2 + 1 - y], from_y.at[k], y_peer)

    def z_copy(k):
        target = lax.rem(z + k, z_size)
        return remote(
            2,
            k - 1,
            y_sums.at[target],
            from_z.at[k - 1],
            {"expert": target * 2 + y, "head": h},
        )

    def core_add(expert):
        core_copy(expert).wait_recv()
        own = partials[aligned(expert * n_head + h, width), :].astype(jnp.float32)
        core_sums[expert] = (own + from_core[expert].astype(jnp.float32)).astype(jnp.bfloat16)

    def y_add(k):
        y_copy(k).wait_recv()
        total = core_sums[k * 2 + y].astype(jnp.float32) + from_y[k].astype(jnp.float32)
        y_sums[k] = total.astype(jnp.bfloat16)

    whole_tiles = group // TILE if group % TILE == 0 else 0
    if not whole_tiles:
        loop(0, full_width // TILE, narrow)

    def scatter_step(k):
        @pl.when(k <= z_size)
        def _():
            target = lax.rem(z + k, z_size)
            if whole_tiles:
                narrow(target, group)
            core_copy(target * 2 + 1 - y).start()
            core_copy(target * 2 + y).start()

        @pl.when(jnp.logical_and(k >= 2, k <= z_size + 1))
        def _():
            target = lax.rem(z + k - 1, z_size)
            core_add(target * 2 + 1 - y)
            y_copy(target).start()
            core_add(target * 2 + y)

        @pl.when(k >= 3)
        def _():
            y_add(lax.rem(z + k - 2, z_size))

            @pl.when(k - 2 < z_size)
            def _():
                z_copy(k - 2).start()

    loop(1, z_size + 3, scatter_step)
    total = stream[aligned(me, width), :].astype(jnp.float32) + y_sums[z].astype(jnp.float32)

    def z_add(k, total):
        z_copy(k).wait_recv()
        return total + from_z[k - 1].astype(jnp.float32)

    total = lax.fori_loop(1, z_size, z_add, total)
    layer_out = total.astype(jnp.bfloat16)
    layer_ref[...] = layer_out
    final_stream[aligned(me, width), :] = layer_out
    clear(lm_squares, logit_total)
    loads[3].wait()
    gather(
        3,
        feature_block(final_stream),
        multiply(final_stream, lm_gain_ref, lm_squares, ((vocab, logit_total),)),
    )

    def summed(k):
        core_copy(k).wait_send()

    loop(0, n_expert, summed)
    loop(0, z_size, lambda k: y_copy(k).wait_send())
    loop(1, z_size, lambda k: z_copy(k).wait_send())

    lm_scale = lax.rsqrt(lm_squares[...] / full_width + 1e-05)

    def project(i):
        columns = aligned(i, TILE)
        logits[columns, :] = (logit_total[:, columns] * lm_scale).T

    for i in range(logits.shape[0] // TILE):
        project(i)
    best = jnp.concatenate(best_of(logits, logits.shape[0] // 8, rows), axis=0)
    candidates[aligned(me, TOPK), :] = best

    def offer(k):
        own = candidates.at[aligned(me, TOPK)]
        return remote(4, k - 1, own, own, device(lax.rem(me + k, n_devices)))

    loop(1, n_devices, lambda k: offer(k).start())
    loop(1, n_devices, lambda k: offer(k).wait_recv())
    best_ref[...] = jnp.concatenate(best_of(candidates, n_devices, rows), axis=0)
    loop(1, n_devices, lambda k: offer(k).wait_send())


def shards(
    hidden_in,
    queries,
    new_keys,
    new_values,
    cache_keys,
    cache_values,
    parents,
    lengths,
    out_proj,
    ffn_gain,
    routes,
    route_weights,
    w_gate,
    w_up,
    w_down,
    lm_gain,
    vocab_weight,
):
    n_head = lax.axis_size("head")
    n_expert = lax.axis_size("expert")
    n_devices = n_expert * n_head
    rows, width = hidden_in.shape
    full_width = width * n_devices
    context = attend(queries, new_keys, new_values, cache_keys, cache_values, parents, lengths)
    in_vmem = pl.BlockSpec(memory_space=pltpu.VMEM)
    in_hbm = pl.BlockSpec(memory_space=pl.ANY)
    half16 = lambda *shape: pltpu.VMEM(shape, jnp.bfloat16)
    layer_t, best_t = pl.pallas_call(
        functools.partial(layer_kernel, n_expert, n_head),
        out_shape=(
            jax.ShapeDtypeStruct((width, rows), jnp.bfloat16),
            jax.ShapeDtypeStruct((TOPK, rows), jnp.float32),
        ),
        in_specs=[in_vmem] * 6 + [in_hbm] * 3 + [in_vmem, in_hbm],
        out_specs=(in_vmem, in_vmem),
        scratch_shapes=[
            half16(*w_gate.shape),
            half16(*w_up.shape),
            half16(*w_down.shape),
            half16(*vocab_weight.shape),
            pltpu.SemaphoreType.DMA((4,)),
            half16(n_head, n_expert * context.shape[0], context.shape[1]),
            half16(full_width, rows),
            half16(full_width, rows),
            pltpu.VMEM((rows, 1), jnp.float32),
            pltpu.VMEM((rows, w_gate.shape[1]), jnp.float32),
            pltpu.VMEM((rows, w_gate.shape[1]), jnp.float32),
            pltpu.VMEM((rows, 1), jnp.float32),
            pltpu.VMEM((rows, vocab_weight.shape[1]), jnp.float32),
            half16(rows, w_gate.shape[1]),
            half16(full_width, rows),
            half16(n_expert, width, rows),
            half16(n_expert, width, rows),
            half16(n_expert // 2, width, rows),
            half16(n_expert // 2, width, rows),
            half16(n_expert // 2, width, rows),
            pltpu.VMEM((vocab_weight.shape[1], rows), jnp.float32),
            pltpu.VMEM((n_devices * TOPK, rows), jnp.float32),
            pltpu.SemaphoreType.DMA((5, n_devices - 1)),
            pltpu.SemaphoreType.DMA((5, n_devices - 1)),
        ],
        compiler_params=pltpu.CompilerParams(
            collective_id=0, has_side_effects=True, vmem_limit_bytes=60 * 2**20
        ),
    )(
        context,
        out_proj.T,
        hidden_in.T,
        ffn_gain.reshape(n_expert // 2, 1, -1),
        routes.T,
        route_weights.T,
        w_gate,
        w_up,
        w_down,
        lm_gain.reshape(n_expert // 2, 1, -1),
        vocab_weight,
    )
    return (layer_t.T, best_t.T)


def solution(mesh):
    placed = (
        P("rep", ("expert", "head")),
        P(("rep", "expert"), "head", None, None),
        P(("rep", "expert"), "head", None),
        P(("rep", "expert"), "head", None),
        P(("rep", "expert"), "head", None, None),
        P(("rep", "expert"), "head", None, None),
        P(("rep", "expert")),
        P(("rep", "expert")),
        P(None, ("expert", "head")),
        P(),
        P("rep", None),
        P("rep", None),
        P(None, ("expert", "head")),
        P(None, ("expert", "head")),
        P(("expert", "head"), None),
        P(),
        P(None, ("expert", "head")),
    )
    return jax.shard_map(
        shards,
        mesh=mesh,
        in_specs=placed,
        out_specs=(P("rep", ("expert", "head")), P("rep", None)),
        check_vma=False,
    )
```
